256 devices in a mesh: dp: 8 (over x_lo, y), tm: 16 (over z, core), height: 2 (over x_hi).
Axes of the slice: x: 4 (x_hi: 2, x_lo: 2; x = x_hi * 2 + x_lo), y: 4, z: 8, core: 2. Of those that a mesh axis runs over, the one named last changes fastest.
Arguments:
- clip_input: bfloat16 [8, 64, 8, 96, 128], P('dp', 'tm', 'height'), may hold values from -6 to 6
- cotangent: bfloat16 [8, 64, 8, 96, 128], P('dp', 'tm', 'height'), may hold values from -6 to 6
- first_kernel: bfloat16 [2592, 96], replicated, may hold values from -0.125 to 0.125
- second_kernel: bfloat16 [2592, 96], replicated, may hold values from -0.125 to 0.125
Outputs:
- block_output: float32 [8, 64, 8, 96, 128], P('dp', 'tm', 'height')
- input_grad: float32 [8, 64, 8, 96, 128], P('dp', 'tm', 'height')
- first_grad: float32 [2592, 96], P('dp')
- second_grad: float32 [2592, 96], P('dp')
The draws below stay inside these ranges and needn't reach their ends.
All inputs are finite; a program needn't handle non-finite values.
Results may differ from the reference program's by a relative error of at most 0.0048.
Values may be sent and summed in bfloat16 or wider, within the bound.
No kernel may reach another device: no remote copies, remote signals or barrier semaphores. Data moves between devices by JAX's collectives and lax.ppermute only.
A program may use at most 64 MiB of HBM per device.

```python
import math
import jax
import jax.numpy as jnp
from jax import lax

C = 96
COLS = 128
CLIPS = 8
FRAMES = 64
ROWS = 8


def shard_levels(rng, shape, pieces, least, largest):
    loudness, own = 1.0, jax.random.fold_in(rng, 6)
    for dim, blocks in pieces:
        heights = jnp.exp(jax.random.uniform(jax.random.fold_in(own, dim), (blocks,), jnp.float32, least / len(pieces), largest / len(pieces)))
        loudness = loudness * jnp.repeat(heights, shape[dim] // blocks).reshape([-1 if axis == dim else 1 for axis in range(len(shape))])
    return loudness


def normal_values(stream_key, shape, width, reach, split=(), kind=jnp.bfloat16):
    values = jax.random.normal(stream_key, shape, jnp.float32) * width
    if len(split) > 0:
        values = shard_levels(stream_key, shape, split, -0.22, 0.18) * values
    return jnp.clip(values, min=-reach, max=reach).astype(kind)


def setup_inputs(seed: int = 0) -> dict:
    seeds = jax.random.split(jax.random.key(seed), 5)
    clip_input = normal_values(seeds[0], (CLIPS, FRAMES, ROWS, C, COLS), 1.0, 6.0, ((0, 8), (1, 16), (2, 2)))
    cotangent = normal_values(seeds[1], (CLIPS, FRAMES, ROWS, C, COLS), 1.0, 6.0, ((0, 8), (1, 16), (2, 2)))
    first_kernel = normal_values(seeds[2], (27 * C, C), (27 * C) ** -0.5, 0.125)
    second_kernel = normal_values(seeds[3], (27 * C, C), (27 * C) ** -0.5, 0.125)
    return dict(clip_input=clip_input, cotangent=cotangent, first_kernel=first_kernel, second_kernel=second_kernel)


EPSILON = 1e-06

def norm_silu(field):
    factor = lax.rsqrt(lax.optimization_barrier(jnp.mean(field * field, axis=2, keepdims=True)) + EPSILON)
    return jax.nn.silu(field * factor)

def conv_clip(field, kernel):
    channels = field.shape[2]
    left_side = jnp.transpose(field, (2, 0, 1, 3))[None]
    right_side = jnp.transpose(kernel.reshape(3, 3, 3, channels, channels), (4, 3, 0, 1, 2))
    result = lax.conv_general_dilated(left_side, right_side, (1, 1, 1), ((2, 0), (1, 1), (1, 1)), precision=lax.Precision.HIGHEST)
    return jnp.transpose(result[0], (1, 2, 0, 3))

def to_bf16_and_back(value):
    return lax.optimization_barrier(value.astype(jnp.bfloat16)).astype(jnp.float32)

def reference(clip_input, cotangent, first_kernel, second_kernel):
    kernel_one = first_kernel.astype(jnp.float32)
    kernel_two = second_kernel.astype(jnp.float32)

    def one_clip(paired):
        source = paired[0].astype(jnp.float32)
        upstream = paired[1].astype(jnp.float32)
        first_act = to_bf16_and_back(norm_silu(source))
        middle = conv_clip(first_act, kernel_one)
        second_act = to_bf16_and_back(norm_silu(middle))
        branch = conv_clip(second_act, kernel_two)
        block_output = source + branch
        unused, pull_two = jax.vjp(conv_clip, second_act, kernel_two)
        second_back, second_term = pull_two(upstream)
        unused, pull_mid = jax.vjp(norm_silu, middle)
        middle_grad = to_bf16_and_back(pull_mid(second_back)[0])
        unused, pull_one = jax.vjp(conv_clip, first_act, kernel_one)
        first_back, first_term = pull_one(middle_grad)
        unused, pull_src = jax.vjp(norm_silu, source)
        input_grad = upstream + pull_src(first_back)[0]
        return (block_output, input_grad, first_term, second_term)
    outputs, grads_in, first_terms, second_terms = lax.map(one_clip, (clip_input, cotangent))
    factor = 1.0 / math.sqrt(CLIPS * FRAMES * ROWS * COLS)
    first_grad = lax.optimization_barrier(jnp.sum(first_terms, axis=0)) * factor
    second_grad = lax.optimization_barrier(jnp.sum(second_terms, axis=0)) * factor
    return (outputs, grads_in, first_grad, second_grad)
```

```python
import math

import jax
import jax.numpy as jnp
from jax import lax
from jax.sharding import Mesh, PartitionSpec as P

EPSILON = 1e-06
TIME = ("z", "core")


def extended_2(array, sides, width):
    for axis, dim in sides:
        peers, length = (lax.axis_size(axis), array.shape[dim])
        up = [(i, (i + 1) % peers) for i in range(peers - 1)]
        down = [(j, i) for i, j in up]
        last = lax.slice_in_dim(array, length - width, length, axis=dim)
        first = lax.slice_in_dim(array, 0, width, axis=dim)
        before = lax.ppermute(last, axis, up)
        after = lax.ppermute(first, axis, down)
        array = jnp.concatenate([before, array, after], axis=dim)
    return array


def passed_along(array, axis, by):
    peers = lax.axis_size(axis)
    pairs = [(i, i + by) for i in range(peers) if 0 <= i + by < peers]
    return lax.ppermute(array, axis, pairs)


def norm_silu(field):
    factor = lax.rsqrt(jnp.mean(field * field, axis=2, keepdims=True) + EPSILON)
    return jax.nn.silu(field * factor)


def pad_rows(extended):
    rimmed = extended_2(extended, (("x_hi", 1),), 1)
    return jnp.pad(rimmed, ((0, 0), (0, 0), (0, 0), (1, 1)))


def time_stack(padded, tap_row, tap_col, frames):
    row_count = padded.shape[1] - 2
    col_count = padded.shape[3] - 2
    window = padded[:, tap_row : tap_row + row_count, :, tap_col : tap_col + col_count]
    return jnp.concatenate([window[offset : offset + frames] for offset in range(3)], axis=2)


def local_conv(padded, kernel, frames):
    channels = padded.shape[2]
    summed = None
    for tap_row in range(3):
        for tap_col in range(3):
            stacked = time_stack(padded, tap_row, tap_col, frames)
            weight = kernel[:, tap_row, tap_col].reshape(3 * channels, kernel.shape[4])
            partial_sum = jnp.einsum(
                "frkw,kd->frdw", stacked, weight, preferred_element_type=jnp.float32
            )
            summed = partial_sum if summed is None else summed + partial_sum
    return summed


def kernel_grad(padded, grad_out, frames):
    channels = padded.shape[2]
    row_list = []
    for tap_row in range(3):
        col_list = []
        for tap_col in range(3):
            stacked = time_stack(padded, tap_row, tap_col, frames)
            piece = jnp.einsum(
                "frkw,frdw->kd", stacked, grad_out, preferred_element_type=jnp.float32
            )
            col_list.append(piece.reshape(3, channels, grad_out.shape[2]))
        row_list.append(jnp.stack(col_list, axis=1))
    gathered = jnp.stack(row_list, axis=1)
    return gathered.reshape(27 * channels, grad_out.shape[2])


def flipped(kernel):
    return jnp.swapaxes(kernel[::-1, ::-1, ::-1], 3, 4)


SWAP = [(0, 1), (1, 0)]
CLIP_AXES = ("x_lo", "y")
PEER_AXES = ("z", "x_hi")


def reduced(first_term, second_term):
    on_first = lax.axis_index("core") == 0
    kept = jnp.where(on_first, first_term, second_term)
    given = jnp.where(on_first, second_term, first_term)
    chip_sum = kept + lax.ppermute(given, "core", SWAP)
    clips = lax.axis_size(CLIP_AXES)
    rows = chip_sum.shape[0] // clips
    pieces = chip_sum.reshape(clips, rows, chip_sum.shape[1]).astype(jnp.bfloat16)
    arrived = lax.all_to_all(pieces, CLIP_AXES, 0, 0, tiled=True)
    clip_sum = jnp.sum(arrived.astype(jnp.float32), axis=0)
    peers = lax.axis_size(PEER_AXES)
    share = -(-rows // (8 * peers)) * 8
    padded = jnp.pad(clip_sum, ((0, share * peers - rows), (0, 0)))
    parts = lax.all_to_all(
        padded.reshape(peers, share, -1), PEER_AXES, 0, 0, tiled=True
    )
    part_sum = jnp.sum(parts, axis=0)
    sent = jnp.broadcast_to(part_sum[None], (peers,) + part_sum.shape)
    whole = lax.all_to_all(sent, PEER_AXES, 0, 0, tiled=True)
    whole = whole.reshape(peers * share, -1)[:rows]
    other = lax.ppermute(whole, "core", SWAP)
    return jnp.where(on_first, whole, other), jnp.where(on_first, other, whole)


def local(clip_input, cotangent, first_kernel, second_kernel):
    frames = clip_input.shape[1]
    channels = clip_input.shape[3]
    source = clip_input[0]
    upstream = cotangent[0]
    kernel_one = first_kernel.reshape(3, 3, 3, channels, channels)
    kernel_two = second_kernel.reshape(3, 3, 3, channels, channels)

    def extend_back(block):
        earlier = passed_along(block[frames - 2 :], TIME, 1)
        return pad_rows(jnp.concatenate([earlier, block], axis=0))

    def extend_ahead(block):
        later = passed_along(block[:2], TIME, -1)
        return pad_rows(jnp.concatenate([block, later], axis=0))

    source_float = source.astype(jnp.float32)
    first_act = norm_silu(source_float).astype(jnp.bfloat16)
    first_padded = extend_back(first_act)
    middle = local_conv(first_padded, kernel_one, frames)
    second_act = norm_silu(middle).astype(jnp.bfloat16)
    second_padded = extend_back(second_act)
    branch = local_conv(second_padded, kernel_two, frames)
    block_output = source_float + branch
    second_back = local_conv(extend_ahead(upstream), flipped(kernel_two), frames)
    unused, pull_mid = jax.vjp(norm_silu, middle)
    middle_grad = pull_mid(second_back)[0].astype(jnp.bfloat16)
    first_back = local_conv(extend_ahead(middle_grad), flipped(kernel_one), frames)
    unused, pull_src = jax.vjp(norm_silu, source_float)
    input_grad = upstream.astype(jnp.float32) + pull_src(first_back)[0]
    positions = (
        frames
        * source.shape[1]
        * source.shape[3]
        * lax.axis_size(("x_lo", "y", "z", "core", "x_hi"))
    )
    factor = 1.0 / math.sqrt(positions)
    first_term = kernel_grad(first_padded, middle_grad, frames) * factor
    second_term = kernel_grad(second_padded, upstream, frames) * factor
    first_grad, second_grad = reduced(first_term, second_term)
    return (block_output[None], input_grad[None], first_grad, second_grad)


def solution(mesh):
    axes = ("x_lo", "y", "z", "core", "x_hi")
    split = Mesh(mesh.devices.reshape(2, 4, 8, 2, 2), axes)
    field = P(CLIP_AXES, TIME, "x_hi", None, None)
    return jax.shard_map(
        local,
        mesh=split,
        in_specs=(field, field, P(), P()),
        out_specs=(field, field, P(CLIP_AXES, None), P(CLIP_AXES, None)),
        check_vma=False,
    )
```

```python
import functools
import math

import jax
import jax.numpy as jnp
from jax import lax
from jax.experimental import pallas as pl
from jax.experimental.pallas import tpu as pltpu
from jax.sharding import Mesh, PartitionSpec as P

EPSILON = 1e-06
TIME = ("z", "core")
CLIP_AXES = ("x_lo", "y")
PEER_AXES = ("z", "x_hi")
HALVES = ("z", "core", "x_hi")
SWAP = [(0, 1), (1, 0)]
BF16, F32 = jnp.bfloat16, jnp.float32

MAIN, STRIP = 256, 80


def sigmoid(u):
    return 1.0 / (1.0 + jnp.exp(-u))


def normed(v):
    scale = lax.rsqrt(jnp.mean(v * v, axis=0, keepdims=True) + EPSILON)
    return v * scale, scale


def norm_silu(v):
    u, _ = normed(v)
    return u * sigmoid(u)


def norm_silu_and_grad(v, back):
    u, scale = normed(v)
    gate = sigmoid(u)
    inner = back * (gate * (1.0 + u * (1.0 - gate)))
    grad = scale * (inner - u * jnp.mean(u * inner, axis=0, keepdims=True))
    return u * gate, grad


def fill(pairs, own, far, side, side_at, own_first, is_upper, change):
    channels, cols = own.shape[2], own.shape[3]
    frames, extra, rows = own.shape[0], far.shape[0], own.shape[1]
    lane = lax.broadcasted_iota(jnp.int32, (channels, cols), 1)
    upper = is_upper.astype(F32)
    own_at, far_at = (0, frames) if own_first else (extra, 0)

    def put(value, frame, row):
        shifted = (
            jnp.where(lane == 0, 0.0, pltpu.roll(value, 1, 1)),
            value,
            jnp.where(lane == cols - 1, 0.0, pltpu.roll(value, cols - 1, 1)),
        )
        for k, part in enumerate(shifted):
            part = part.astype(BF16)
            band = pl.ds(k * channels, channels)
            if frame < frames:
                pairs[frame, row, band, pl.ds(0, cols)] = part
            if frame >= 2:
                pairs[frame - 2, row, band, pl.ds(cols, cols)] = part

    for field, base in ((own, own_at), (far, far_at)):
        for f in range(field.shape[0]):

            @pl.loop(0, rows)
            def _(r):
                put(change(field[f, r].astype(F32)), base + f, r + 1)

            edge = side[side_at + f] if field is own else far[f, rows]
            value = change(edge.astype(F32))
            put(value * (1.0 - upper), base + f, 0)
            put(value * upper, base + f, rows + 1)


def conv_pair(weight, pairs, f, r):
    stacked = jnp.concatenate(
        [pairs[f + kt, pl.ds(r, 3)].reshape(-1, pairs.shape[3]) for kt in range(3)], axis=0
    )
    return jnp.dot(weight[...], stacked, preferred_element_type=F32)


def nt_dot(left, right):
    return lax.dot_general(left, right, (((1,), (1,)), ((), ())), preferred_element_type=F32)


def head_kernel(
    scale, owners, flags, x, x_far, c, c_far, side, w_one, w_two_back,
    act_out, grad_out, side_out, kept, given, px, pc, lanes_act, lanes_grad, sums,
):
    frames, rows, channels, cols = x.shape
    is_upper, core = flags[0] == 0, flags[1]
    fill(px, x, x_far, side, 0, False, is_upper, norm_silu)
    fill(pc, c, c_far, side, frames, True, is_upper, lambda v: v)

    for f in range(frames // 2):

        @pl.loop(0, rows)
        def _(r):
            middle = conv_pair(w_one, px, f, r)
            back = conv_pair(w_two_back, pc, f, r)
            act, grad = norm_silu_and_grad(middle, back)
            act, grad = act.astype(BF16), grad.astype(BF16)
            spot = f * rows + r
            lanes_act[spot] = act
            lanes_grad[spot] = grad
            for half in range(2):
                part = pl.ds(half * cols, cols)
                act_out[f + 2 * half, r] = act[:, half * cols : (half + 1) * cols]
                grad_out[f + 2 * half, r] = grad[:, half * cols : (half + 1) * cols]

    edge = jnp.where(is_upper, rows - 1, 0)
    for f in range(frames):
        side_out[f] = act_out[f, edge]
        side_out[frames + f] = grad_out[f, edge]

    spots = [(f, r) for f in range(frames // 2) for r in range(rows)]
    taps = 3 * channels

    @pl.loop(0, 9)
    def _(k):
        kt, kh = k // 3, k % 3
        left = jnp.concatenate([px[f + kt, r + kh] for f, r in spots], axis=1)
        right = jnp.concatenate([lanes_grad[i] for i in range(len(spots))], axis=1)
        first = pl.multiple_of(k * taps, 8)
        sums[0, pl.ds(first, taps), pl.ds(0, channels)] = nt_dot(left, right)

    @pl.loop(0, 9)
    def _(k):
        kt, kh = k // 3, k % 3
        left = jnp.concatenate([lanes_act[i] for i in range(len(spots))], axis=1)
        right = jnp.concatenate([pc[f + kt, r + kh] for f, r in spots], axis=1)
        product = nt_dot(left, right)
        for kw in range(3):
            tap = 26 - (3 * k + kw)
            first = pl.multiple_of(tap * channels, 8)
            sums[1, pl.ds(first, channels), pl.ds(0, channels)] = product[:, kw * channels : (kw + 1) * channels]

    total = 27 * channels
    sums[:, pl.ds(total, sums.shape[1] - total), :] = jnp.zeros((2, sums.shape[1] - total, cols), F32)
    share = total // owners
    lane = lax.broadcasted_iota(jnp.int32, (STRIP, cols), 1)
    for target, source in ((kept, core), (given, 1 - core)):
        for d in range(owners):
            rest = sums[source, pl.ds(share * d + MAIN, STRIP), :]
            for s in range(4):
                height = min(STRIP, MAIN - s * STRIP)
                main = sums[source, pl.ds(share * d + s * STRIP, height), :]
                if s < 3:
                    strip = pltpu.roll(rest, 96 - 32 * s, 1)
                else:
                    strip = jnp.zeros((STRIP, cols), F32)
                mixed = jnp.where(lane[:height] < channels, main, strip[:height])
                target[d, pl.ds(s * STRIP, height), :] = mixed * scale


def branch_kernel(flags, x, act, a_far, side, w_two, block_out, pa):
    frames, rows, channels, cols = x.shape
    fill(pa, act, a_far, side, 0, False, flags[0] == 0, lambda v: v)
    for f in range(frames // 2):

        @pl.loop(0, rows)
        def _(r):
            branch = conv_pair(w_two, pa, f, r)
            for half in range(2):
                part = slice(half * cols, (half + 1) * cols)
                at = f + 2 * half
                block_out[at, r] = x[at, r].astype(F32) + branch[:, part]


def input_kernel(flags, x, c, grad, g_far, side, w_one_back, input_out, pg):
    frames, rows, channels, cols = x.shape
    fill(pg, grad, g_far, side, frames, True, flags[0] == 0, lambda v: v)
    for f in range(frames // 2):

        @pl.loop(0, rows)
        def _(r):
            back = conv_pair(w_one_back, pg, f, r)
            for half in range(2):
                part = slice(half * cols, (half + 1) * cols)
                at = f + 2 * half
                _, grad_in = norm_silu_and_grad(x[at, r].astype(F32), back[:, part])
                input_out[at, r] = c[at, r].astype(F32) + grad_in


def weights_kernel(first, second, w_one, w_two_back, w_two, w_one_back):
    channels = first.shape[1]
    for source, ahead, back in ((first, w_one, w_one_back), (second, w_two, w_two_back)):
        ahead[...] = source[...].astype(F32).T.astype(BF16)
        taps = [source[pl.ds((26 - t) * channels, channels), :].astype(F32) for t in range(27)]
        back[...] = jnp.concatenate(taps, axis=1).astype(BF16)


def weights(first, second):
    turned = jax.ShapeDtypeStruct(first.shape[::-1], BF16)
    vmem = pl.BlockSpec(memory_space=pltpu.VMEM)
    return pl.pallas_call(
        weights_kernel,
        out_shape=(turned,) * 4,
        in_specs=[vmem] * 2,
        out_specs=[vmem] * 4,
        compiler_params=pltpu.CompilerParams(vmem_limit_bytes=24 * 1024 * 1024),
        cost_estimate=pl.CostEstimate(flops=3 * 10**9, bytes_accessed=6 * first.size, transcendentals=0),
    )(first, second)


def call(kernel, outs, scratch, flops, args):
    vmem = pl.BlockSpec(memory_space=pltpu.VMEM)
    moved = sum(a.size * a.dtype.itemsize for a in list(args[1:]) + list(outs))
    return pl.pallas_call(
        kernel,
        out_shape=outs,
        in_specs=[pl.BlockSpec(memory_space=pltpu.SMEM)] + [vmem] * (len(args) - 1),
        out_specs=[vmem] * len(outs),
        scratch_shapes=scratch,
        compiler_params=pltpu.CompilerParams(vmem_limit_bytes=24 * 1024 * 1024),
        cost_estimate=pl.CostEstimate(flops=flops, bytes_accessed=moved, transcendentals=0),
    )(*args)


def halos(earlier, later, side):
    frames = earlier.shape[0]
    peers = lax.axis_size(TIME)
    ahead = [(i, i + 1) for i in range(peers - 1)]
    behind = [(j, i) for i, j in ahead]
    edge = lax.ppermute(side, "x_hi", SWAP)
    last = jnp.concatenate([earlier[frames - 2 :], edge[frames - 2 : frames, None]], axis=1)
    first = jnp.concatenate([later[:2], edge[frames : frames + 2, None]], axis=1)
    far_a = lax.ppermute(last, TIME, ahead)
    far_b = lax.ppermute(first, TIME, behind)
    return far_a, far_b, edge


def clip_total(kept, given):
    pieces = (kept + lax.ppermute(given, "core", SWAP)).astype(BF16)
    arrived = lax.all_to_all(pieces, CLIP_AXES, 0, 0, tiled=True)
    return jnp.sum(arrived.astype(F32), axis=0)


def exchanged(parts):
    return lax.all_to_all(parts, PEER_AXES, 0, 0, tiled=True)


def unpacked(packed, share, channels):
    left = share - MAIN
    strips = [packed[s * STRIP : s * STRIP + left, channels:] for s in range(3)]
    return jnp.concatenate([packed[:, :channels], jnp.concatenate(strips, axis=1)], axis=0)


def local(clip_input, cotangent, first_kernel, second_kernel):
    source, upstream = clip_input[0], cotangent[0]
    frames, rows, channels, cols = source.shape
    half, core = lax.axis_index("x_hi"), lax.axis_index("core")
    flags = jnp.stack([half, core]).astype(jnp.int32)
    edge = jnp.where(half == 0, rows - 1, 0)
    side = jnp.concatenate(
        [lax.dynamic_index_in_dim(a, edge, 1, keepdims=False) for a in (source, upstream)], axis=0
    )
    w_one, w_two_back, w_two, w_one_back = weights(first_kernel, second_kernel)
    x_far, c_far, side = halos(source, upstream, side)

    owners = lax.axis_size(CLIP_AXES)
    positions = frames * rows * cols * lax.axis_size(CLIP_AXES + HALVES)
    field = jax.ShapeDtypeStruct(source.shape, BF16)
    packed = jax.ShapeDtypeStruct((owners, MAIN, cols), F32)
    pairs = pltpu.VMEM((frames, rows + 2, 3 * channels, 2 * cols), BF16)
    spots = frames * rows // 2
    conv_flops = 2 * 27 * channels * channels * frames * rows * cols
    act, grad, side, kept, given = call(
        functools.partial(head_kernel, 1.0 / math.sqrt(positions), owners),
        (field, field, jax.ShapeDtypeStruct((2 * frames, channels, cols), BF16), packed, packed),
        [
            pairs,
            pairs,
            pltpu.VMEM((spots, channels, 2 * cols), BF16),
            pltpu.VMEM((spots, channels, 2 * cols), BF16),
            pltpu.VMEM((2, 27 * channels + 32, cols), F32),
        ],
        4 * conv_flops,
        (flags, source, x_far, upstream, c_far, side, w_one, w_two_back),
    )
    out = jax.ShapeDtypeStruct(source.shape, F32)
    peers = lax.axis_size(PEER_AXES)
    a_far, g_far, side = halos(act, grad, side)
    clip_sum = clip_total(kept, given)
    clip_sum, a_far, g_far, side = lax.optimization_barrier((clip_sum, a_far, g_far, side))
    parts = exchanged(clip_sum.reshape(peers, MAIN // peers, -1))
    (block_output,) = call(
        branch_kernel, (out,), [pairs], conv_flops, (flags, source, act, a_far, side, w_two)
    )
    parts, block_output, g_far, side = lax.optimization_barrier((parts, block_output, g_far, side))
    part_sum = jnp.sum(parts, axis=0)
    sent = jnp.broadcast_to(part_sum[None], (peers,) + part_sum.shape)
    sent, g_far, side = lax.optimization_barrier((sent, g_far, side))
    whole = exchanged(sent).reshape(MAIN, -1)
    (input_grad,) = call(
        input_kernel, (out,), [pairs], conv_flops, (flags, source, upstream, grad, g_far, side, w_one_back)
    )
    whole, input_grad = lax.optimization_barrier((whole, input_grad))
    other = lax.ppermute(whole, "core", SWAP)
    first_packed = jnp.where(core == 0, whole, other)
    second_packed = jnp.where(core == 0, other, whole)
    share = 27 * channels // owners
    return (
        block_output[None],
        input_grad[None],
        unpacked(first_packed, share, channels),
        unpacked(second_packed, share, channels),
    )


def solution(mesh):
    shape = mesh.shape
    axes = CLIP_AXES + TIME + ("x_hi",)
    split = Mesh(mesh.devices.reshape(2, shape["dp"] // 2, shape["tm"] // 2, 2, shape["height"]), axes)
    field = P(CLIP_AXES, TIME, "x_hi", None, None)
    return jax.shard_map(
        local,
        mesh=split,
        in_specs=(field, field, P(), P()),
        out_specs=(field, field, P(CLIP_AXES, None), P(CLIP_AXES, None)),
        check_vma=False,
    )
```

```python
import functools
import math

import jax
import jax.numpy as jnp
from jax import lax
from jax.experimental import pallas as pl
from jax.experimental.pallas import tpu as pltpu
from jax.sharding import Mesh, PartitionSpec as P

EPSILON = 1e-06
TIME = ("z", "core")
CLIP_AXES = ("x_lo", "y")
PEER_AXES = ("z", "x_hi")
HALVES = ("z", "core", "x_hi")
SWAP = [(0, 1), (1, 0)]
BF16, F32 = jnp.bfloat16, jnp.float32

MAIN, STRIP = 256, 80


def sigmoid(u):
    return 0.5 + 0.5 * jnp.tanh(0.5 * u)


def normed(v):
    scale = lax.rsqrt(jnp.mean(v * v, axis=0, keepdims=True) + EPSILON)
    return v * scale, scale


def norm_silu(v):
    u, _ = normed(v)
    return u * sigmoid(u)


def norm_silu_and_grad(v, back):
    u, scale = normed(v)
    gate = sigmoid(u)
    inner = back * (gate * (1.0 + u * (1.0 - gate)))
    grad = scale * (inner - u * jnp.mean(u * inner, axis=0, keepdims=True))
    return u * gate, grad


def fill(pairs, own, far, side, side_at, own_first, is_upper, change):
    frames, extra, rows, cols = own.shape[0], far.shape[0], own.shape[1], own.shape[3]
    upper = is_upper.astype(F32)
    own_at, far_at = (0, frames) if own_first else (extra, 0)

    def put(value, frame, row):
        value = value.astype(BF16)
        if frame < frames:
            pairs[frame, row, :, pl.ds(0, cols)] = value
        if frame >= 2:
            pairs[frame - 2, row, :, pl.ds(cols, cols)] = value

    for field, base in ((own, own_at), (far, far_at)):
        for f in range(field.shape[0]):
            for r in range(rows):
                put(change(field[f, r].astype(F32)), base + f, r + 1)
            edge = side[side_at + f] if field is own else far[f, rows]
            value = change(edge.astype(F32))
            put(value * (1.0 - upper), base + f, 0)
            put(value * upper, base + f, rows + 1)


def shifted(value, by):
    cols = value.shape[1]
    lane = lax.broadcasted_iota(jnp.int32, value.shape, 1)
    return jnp.where(lane == (0 if by == 1 else cols - 1), 0.0, pltpu.roll(value, by % cols, 1))


def halves(value):
    cols = value.shape[1] // 2
    return value[:, :cols], value[:, cols:]


def conv_pair(weight, pairs, f, r):
    channels = pairs.shape[2]
    stacked = jnp.concatenate(
        [pairs[f + kt, pl.ds(r, 3)].reshape(3 * channels, -1) for kt in range(3)], axis=0
    )
    product = jnp.dot(weight[...], stacked, preferred_element_type=F32)
    return jnp.concatenate(
        [
            shifted(part[:channels], 1) + part[channels : 2 * channels] + shifted(part[2 * channels :], -1)
            for part in halves(product)
        ],
        axis=1,
    )


def put_shifts(target, spot, value):
    channels = value.shape[0]
    cols = value.shape[1] // 2
    for half, part in enumerate(halves(value)):
        lanes = pl.ds(half * cols, cols)
        for k, by in ((0, -1), (1, 0), (2, 1)):
            moved = shifted(part, by) if by else part
            target[spot, pl.ds(k * channels, channels), lanes] = moved.astype(BF16)


def nt_dot(left, right):
    return lax.dot_general(left, right, (((1,), (1,)), ((), ())), preferred_element_type=F32)


def head_kernel(
    scale, owners, flags, x, x_far, c, c_far, side, w_one, w_two_back,
    act_out, grad_out, side_out, kept, given, px, pc, lanes_act, lanes_grad, sums,
):
    frames, rows, channels, cols = x.shape
    is_upper, core = flags[0] == 0, flags[1]
    fill(px, x, x_far, side, 0, False, is_upper, norm_silu)
    fill(pc, c, c_far, side, frames, True, is_upper, lambda v: v)

    for f in range(frames // 2):

        @pl.loop(0, rows, unroll=True)
        def _(r):
            middle = conv_pair(w_one, px, f, r)
            back = conv_pair(w_two_back, pc, f, r)
            act, grad = norm_silu_and_grad(middle, back)
            spot = f * rows + r
            put_shifts(lanes_act, spot, act)
            put_shifts(lanes_grad, spot, grad)
            for half in range(2):
                act_out[f + 2 * half, r] = act[:, half * cols : (half + 1) * cols].astype(BF16)
                grad_out[f + 2 * half, r] = grad[:, half * cols : (half + 1) * cols].astype(BF16)

    edge = jnp.where(is_upper, rows - 1, 0)
    for f in range(frames):
        side_out[f] = act_out[f, edge]
        side_out[frames + f] = grad_out[f, edge]

    spots = [(f, r) for f in range(frames // 2) for r in range(rows)]
    taps = 3 * channels

    def lined(scratch):
        return jnp.concatenate([scratch[i] for i in range(len(spots))], axis=1)

    def padded(pairs, kt):
        return jnp.concatenate([pairs[f + kt, pl.ds(r, 3)].reshape(taps, -1) for f, r in spots], axis=1)

    @pl.loop(0, 3, unroll=True)
    def _(kt):
        product = nt_dot(padded(px, kt), lined(lanes_grad))
        for kh in range(3):
            for kw in range(3):
                first = pl.multiple_of((9 * kt + 3 * kh + kw) * channels, 8)
                block = product[kh * channels : (kh + 1) * channels, kw * channels : (kw + 1) * channels]
                sums[0, pl.ds(first, channels), pl.ds(0, channels)] = block

    @pl.loop(0, 3, unroll=True)
    def _(kt):
        product = nt_dot(lined(lanes_act), padded(pc, kt))
        for kh in range(3):
            for kw in range(3):
                first = pl.multiple_of((26 - (9 * kt + 3 * kh + kw)) * channels, 8)
                block = product[kw * channels : (kw + 1) * channels, kh * channels : (kh + 1) * channels]
                sums[1, pl.ds(first, channels), pl.ds(0, channels)] = block

    total = 27 * channels
    sums[:, pl.ds(total, sums.shape[1] - total), :] = jnp.zeros((2, sums.shape[1] - total, cols), F32)
    share = total // owners
    lane = lax.broadcasted_iota(jnp.int32, (STRIP, cols), 1)
    for target, source in ((kept, core), (given, 1 - core)):
        for d in range(owners):
            rest = sums[source, pl.ds(share * d + MAIN, STRIP), :]
            for s in range(4):
                height = min(STRIP, MAIN - s * STRIP)
                main = sums[source, pl.ds(share * d + s * STRIP, height), :]
                if s < 3:
                    strip = pltpu.roll(rest, 96 - 32 * s, 1)
                else:
                    strip = jnp.zeros((STRIP, cols), F32)
                mixed = jnp.where(lane[:height] < channels, main, strip[:height])
                target[d, pl.ds(s * STRIP, height), :] = mixed * scale


def branch_kernel(flags, x, act, a_far, side, w_two, block_out, pa):
    frames, rows, channels, cols = x.shape
    fill(pa, act, a_far, side, 0, False, flags[0] == 0, lambda v: v)
    for f in range(frames // 2):

        @pl.loop(0, rows, unroll=True)
        def _(r):
            branch = conv_pair(w_two, pa, f, r)
            for half in range(2):
                part = slice(half * cols, (half + 1) * cols)
                at = f + 2 * half
                block_out[at, r] = x[at, r].astype(F32) + branch[:, part]


def input_kernel(flags, x, c, grad, g_far, side, w_one_back, input_out, pg):
    frames, rows, channels, cols = x.shape
    fill(pg, grad, g_far, side, frames, True, flags[0] == 0, lambda v: v)
    for f in range(frames // 2):

        @pl.loop(0, rows, unroll=True)
        def _(r):
            back = conv_pair(w_one_back, pg, f, r)
            for half in range(2):
                part = slice(half * cols, (half + 1) * cols)
                at = f + 2 * half
                _, grad_in = norm_silu_and_grad(x[at, r].astype(F32), back[:, part])
                input_out[at, r] = c[at, r].astype(F32) + grad_in


def weights_kernel(first, second, w_one, w_two_back, w_two, w_one_back):
    channels = first.shape[0]
    for source, ahead, back in ((first, w_one, w_one_back), (second, w_two, w_two_back)):
        whole = source[...].astype(F32)
        taps = [whole[:, t * channels : (t + 1) * channels] for t in range(27)]
        for kw in range(3):
            rows = pl.ds(kw * channels, channels)
            ahead[rows, :] = jnp.concatenate([taps[3 * k + kw] for k in range(9)], axis=1).astype(BF16)
            back[rows, :] = jnp.concatenate([taps[26 - 3 * k - kw].T for k in range(9)], axis=1).astype(BF16)


def weights(first, second):
    turned = jax.ShapeDtypeStruct((3 * first.shape[0], first.shape[1] // 3), BF16)
    vmem = pl.BlockSpec(memory_space=pltpu.VMEM)
    return pl.pallas_call(
        weights_kernel,
        out_shape=(turned,) * 4,
        in_specs=[vmem] * 2,
        out_specs=[vmem] * 4,
        compiler_params=pltpu.CompilerParams(vmem_limit_bytes=10 * 1024 * 1024),
        cost_estimate=pl.CostEstimate(flops=3 * 10**9, bytes_accessed=6 * first.size, transcendentals=0),
    )(first, second)


def call(kernel, outs, scratch, flops, args, mib=12):
    vmem = pl.BlockSpec(memory_space=pltpu.VMEM)
    moved = sum(a.size * a.dtype.itemsize for a in list(args[1:]) + list(outs))
    return pl.pallas_call(
        kernel,
        out_shape=outs,
        in_specs=[pl.BlockSpec(memory_space=pltpu.SMEM)] + [vmem] * (len(args) - 1),
        out_specs=[vmem] * len(outs),
        scratch_shapes=scratch,
        compiler_params=pltpu.CompilerParams(vmem_limit_bytes=mib * 1024 * 1024),
        cost_estimate=pl.CostEstimate(flops=flops, bytes_accessed=moved, transcendentals=0),
    )(*args)


def halos(earlier, later, side):
    frames = earlier.shape[0]
    peers = lax.axis_size(TIME)
    ahead = [(i, i + 1) for i in range(peers - 1)]
    behind = [(j, i) for i, j in ahead]
    edge = lax.ppermute(side, "x_hi", SWAP)
    last = jnp.concatenate([earlier[frames - 2 :], edge[frames - 2 : frames, None]], axis=1)
    first = jnp.concatenate([later[:2], edge[frames : frames + 2, None]], axis=1)
    far_a = lax.ppermute(last, TIME, ahead)
    far_b = lax.ppermute(first, TIME, behind)
    return far_a, far_b, edge


def chip_total(kept, given):
    return (kept + lax.ppermute(given, "core", SWAP)).astype(BF16)


def clip_total(pieces):
    arrived = lax.all_to_all(pieces, CLIP_AXES, 0, 0, tiled=True)
    total = jax.ShapeDtypeStruct(pieces.shape[1:], F32)
    return small_call(total_kernel, (total,), (arrived,), False)[0]


def exchanged(parts):
    return lax.all_to_all(parts, PEER_AXES, 0, 0, tiled=True)


def total_kernel(arrived, total):
    acc = arrived[0].astype(F32)
    for d in range(1, arrived.shape[0]):
        acc = acc + arrived[d].astype(F32)
    total[...] = acc


def unpack_kernel(flags, whole, other, first, second):
    channels, share = first.shape
    left = share - MAIN
    cols = whole.shape[1]

    def write(target, packed):
        target[:, pl.ds(0, MAIN)] = packed[...].T[:channels]
        lane = lax.broadcasted_iota(jnp.int32, (STRIP, cols), 1)
        width = cols - channels
        strips = [pltpu.roll(packed[pl.ds(s * STRIP, STRIP), :], (s + 1) * width, 1) for s in range(3)]
        rest = jnp.where(lane < width, strips[0], jnp.where(lane < 2 * width, strips[1], strips[2]))
        target[:, pl.ds(MAIN, left)] = rest.T[:channels, :left]

    for core, pair in ((0, (first, second)), (1, (second, first))):

        @pl.when(flags[1] == core)
        def _():
            write(pair[0], whole)
            write(pair[1], other)


def small_call(kernel, outs, args, flagged):
    vmem = pl.BlockSpec(memory_space=pltpu.VMEM)
    moved = sum(a.size * a.dtype.itemsize for a in list(args) + list(outs))
    specs = [vmem] * len(args)
    if flagged:
        specs[0] = pl.BlockSpec(memory_space=pltpu.SMEM)
    return pl.pallas_call(
        kernel,
        out_shape=outs,
        in_specs=specs,
        out_specs=[vmem] * len(outs),
        compiler_params=pltpu.CompilerParams(vmem_limit_bytes=4 * 1024 * 1024),
        cost_estimate=pl.CostEstimate(flops=0, bytes_accessed=moved, transcendentals=0),
    )(*args)


def head(source, x_far, upstream, c_far, side, w_one, w_two_back, flags, owners, scale):
    frames, rows, channels, cols = source.shape
    field = jax.ShapeDtypeStruct(source.shape, BF16)
    packed = jax.ShapeDtypeStruct((owners, MAIN, cols), F32)
    pairs = pltpu.VMEM((frames, rows + 2, channels, 2 * cols), BF16)
    spots = frames * rows // 2
    conv_flops = 2 * 27 * channels * channels * frames * rows * cols
    return call(
        functools.partial(head_kernel, scale, owners),
        (field, field, jax.ShapeDtypeStruct((2 * frames, channels, cols), BF16), packed, packed),
        [
            pairs,
            pairs,
            pltpu.VMEM((spots, 3 * channels, 2 * cols), BF16),
            pltpu.VMEM((spots, 3 * channels, 2 * cols), BF16),
            pltpu.VMEM((2, 27 * channels + 32, cols), F32),
        ],
        4 * conv_flops,
        (flags, source, x_far, upstream, c_far, side, w_one, w_two_back),
        mib=22,
    )


def local(clip_input, cotangent, first_kernel, second_kernel):
    source, upstream = clip_input[0], cotangent[0]
    frames, rows, channels, cols = source.shape
    half, core = lax.axis_index("x_hi"), lax.axis_index("core")
    flags = jnp.stack([half, core]).astype(jnp.int32)
    edge = jnp.where(half == 0, rows - 1, 0)
    side = jnp.concatenate(
        [lax.dynamic_index_in_dim(a, edge, 1, keepdims=False) for a in (source, upstream)], axis=0
    )
    w_one, w_two_back, w_two, w_one_back = weights(first_kernel.T, second_kernel.T)
    x_far, c_far, side = halos(source, upstream, side)

    owners = lax.axis_size(CLIP_AXES)
    positions = frames * rows * cols * lax.axis_size(CLIP_AXES + HALVES)
    act, grad, side, kept, given = head(
        source, x_far, upstream, c_far, side, w_one, w_two_back, flags, owners, 1.0 / math.sqrt(positions)
    )
    pairs = pltpu.VMEM((frames, rows + 2, channels, 2 * cols), BF16)
    conv_flops = 2 * 27 * channels * channels * frames * rows * cols
    out = jax.ShapeDtypeStruct(source.shape, F32)
    peers = lax.axis_size(PEER_AXES)
    pieces, side = lax.optimization_barrier((chip_total(kept, given), side))
    clip_sum = clip_total(pieces)
    a_far, g_far, side = halos(act, grad, side)
    clip_sum, a_far, g_far, side = lax.optimization_barrier((clip_sum, a_far, g_far, side))
    parts = exchanged(clip_sum.reshape(peers, MAIN // peers, -1))
    (block_output,) = call(
        branch_kernel, (out,), [pairs], conv_flops, (flags, source, act, a_far, side, w_two)
    )
    parts, block_output, g_far, side = lax.optimization_barrier((parts, block_output, g_far, side))
    part_sum = jnp.sum(parts, axis=0)
    sent = jnp.broadcast_to(part_sum[None], (peers,) + part_sum.shape)
    sent, g_far, side = lax.optimization_barrier((sent, g_far, side))
    whole = exchanged(sent).reshape(MAIN, -1)
    (input_grad,) = call(
        input_kernel, (out,), [pairs], conv_flops, (flags, source, upstream, grad, g_far, side, w_one_back)
    )
    whole, input_grad = lax.optimization_barrier((whole, input_grad))
    other = lax.ppermute(whole, "core", SWAP)
    owned = jax.ShapeDtypeStruct((channels, 27 * channels // owners), F32)
    first_grad, second_grad = small_call(unpack_kernel, (owned, owned), (flags, whole, other), True)
    return (
        block_output[None],
        input_grad[None],
        first_grad.T,
        second_grad.T,
    )


def solution(mesh):
    shape = mesh.shape
    axes = CLIP_AXES + TIME + ("x_hi",)
    split = Mesh(mesh.devices.reshape(2, shape["dp"] // 2, shape["tm"] // 2, 2, shape["height"]), axes)
    field = P(CLIP_AXES, TIME, "x_hi", None, None)
    return jax.shard_map(
        local,
        mesh=split,
        in_specs=(field, field, P(), P()),
        out_specs=(field, field, P(CLIP_AXES, None), P(CLIP_AXES, None)),
        check_vma=False,
    )
```

```python
import functools
import math

import jax
import jax.numpy as jnp
from jax import lax
from jax.experimental import pallas as pl
from jax.experimental.pallas import tpu as pltpu
from jax.sharding import Mesh, PartitionSpec as P

EPSILON = 1e-06
TIME = ("z", "core")
CLIP_AXES = ("x_lo", "y")
HALVES = ("z", "core", "x_hi")
SWAP = [(0, 1), (1, 0)]
BF16, F32 = jnp.bfloat16, jnp.float32

MAIN, STRIP = 256, 80


def sigmoid(u):
    return 0.5 + 0.5 * jnp.tanh(0.5 * u)


def normed(v):
    scale = lax.rsqrt(jnp.mean(v * v, axis=0, keepdims=True) + EPSILON)
    return v * scale, scale


def norm_silu(v):
    u, _ = normed(v)
    return u * sigmoid(u)


def norm_silu_and_grad(v, back):
    u, scale = normed(v)
    gate = sigmoid(u)
    inner = back * (gate * (1.0 + u * (1.0 - gate)))
    grad = scale * (inner - u * jnp.mean(u * inner, axis=0, keepdims=True))
    return u * gate, grad


def fill(pairs, own, far, side, side_at, own_first, is_upper, change):
    frames, extra, rows, cols = own.shape[0], far.shape[0], own.shape[1], own.shape[3]
    upper = is_upper.astype(F32)
    own_at, far_at = (0, frames) if own_first else (extra, 0)

    def put(value, frame, row):
        value = value.astype(BF16)
        if frame < frames:
            pairs[frame, row, :, pl.ds(0, cols)] = value
        if frame >= 2:
            pairs[frame - 2, row, :, pl.ds(cols, cols)] = value

    for field, base in ((own, own_at), (far, far_at)):
        for f in range(field.shape[0]):
            for r in range(rows):
                put(change(field[f, r].astype(F32)), base + f, r + 1)
            edge = side[side_at + f] if field is own else far[f, rows]
            value = change(edge.astype(F32))
            put(value * (1.0 - upper), base + f, 0)
            put(value * upper, base + f, rows + 1)


def shifted(value, by):
    cols = value.shape[1]
    lane = lax.broadcasted_iota(jnp.int32, value.shape, 1)
    return jnp.where(lane == (0 if by == 1 else cols - 1), 0.0, pltpu.roll(value, by % cols, 1))


def halves(value):
    cols = value.shape[1] // 2
    return value[:, :cols], value[:, cols:]


def conv_pair(weight, pairs, f, r):
    channels = pairs.shape[2]
    stacked = jnp.concatenate(
        [pairs[f + kt, pl.ds(r, 3)].reshape(3 * channels, -1) for kt in range(3)], axis=0
    )
    product = jnp.dot(weight[...], stacked, preferred_element_type=F32)
    return jnp.concatenate(
        [
            shifted(part[:channels], 1) + part[channels : 2 * channels] + shifted(part[2 * channels :], -1)
            for part in halves(product)
        ],
        axis=1,
    )


def put_shifts(target, spot, value):
    channels = value.shape[0]
    cols = value.shape[1] // 2
    for half, part in enumerate(halves(value)):
        lanes = pl.ds(half * cols, cols)
        for k, by in ((0, -1), (1, 0), (2, 1)):
            moved = shifted(part, by) if by else part
            target[spot, pl.ds(k * channels, channels), lanes] = moved.astype(BF16)


def nt_dot(left, right):
    return lax.dot_general(left, right, (((1,), (1,)), ((), ())), preferred_element_type=F32)


def head_kernel(
    scale, owners, flags, x, x_far, c, c_far, side, w_one, w_two_back,
    act_out, grad_out, side_out, kept, given, px, pc, lanes_act, lanes_grad, sums,
):
    frames, rows, channels, cols = x.shape
    is_upper, core = flags[0] == 0, flags[1]
    fill(px, x, x_far, side, 0, False, is_upper, norm_silu)
    fill(pc, c, c_far, side, frames, True, is_upper, lambda v: v)

    for f in range(frames // 2):

        @pl.loop(0, rows, unroll=True)
        def _(r):
            middle = conv_pair(w_one, px, f, r)
            back = conv_pair(w_two_back, pc, f, r)
            act, grad = norm_silu_and_grad(middle, back)
            spot = f * rows + r
            put_shifts(lanes_act, spot, act)
            put_shifts(lanes_grad, spot, grad)
            for half in range(2):
                act_out[f + 2 * half, r] = act[:, half * cols : (half + 1) * cols].astype(BF16)
                grad_out[f + 2 * half, r] = grad[:, half * cols : (half + 1) * cols].astype(BF16)

    edge = jnp.where(is_upper, rows - 1, 0)
    for f in range(frames):
        side_out[f] = act_out[f, edge]
        side_out[frames + f] = grad_out[f, edge]

    spots = [(f, r) for f in range(frames // 2) for r in range(rows)]
    taps = 3 * channels

    def lined(scratch):
        return jnp.concatenate([scratch[i] for i in range(len(spots))], axis=1)

    def padded(pairs, kt):
        return jnp.concatenate([pairs[f + kt, pl.ds(r, 3)].reshape(taps, -1) for f, r in spots], axis=1)

    @pl.loop(0, 3, unroll=True)
    def _(kt):
        product = nt_dot(padded(px, kt), lined(lanes_grad))
        for kh in range(3):
            for kw in range(3):
                first = pl.multiple_of((9 * kt + 3 * kh + kw) * channels, 8)
                block = product[kh * channels : (kh + 1) * channels, kw * channels : (kw + 1) * channels]
                sums[0, pl.ds(first, channels), pl.ds(0, channels)] = block

    @pl.loop(0, 3, unroll=True)
    def _(kt):
        product = nt_dot(lined(lanes_act), padded(pc, kt))
        for kh in range(3):
            for kw in range(3):
                first = pl.multiple_of((26 - (9 * kt + 3 * kh + kw)) * channels, 8)
                block = product[kw * channels : (kw + 1) * channels, kh * channels : (kh + 1) * channels]
                sums[1, pl.ds(first, channels), pl.ds(0, channels)] = block

    total = 27 * channels
    sums[:, pl.ds(total, sums.shape[1] - total), :] = jnp.zeros((2, sums.shape[1] - total, cols), F32)
    share = total // owners
    lane = lax.broadcasted_iota(jnp.int32, (STRIP, cols), 1)
    for target, source in ((kept, core), (given, 1 - core)):
        for d in range(owners):
            rest = sums[source, pl.ds(share * d + MAIN, STRIP), :]
            for s in range(4):
                height = min(STRIP, MAIN - s * STRIP)
                main = sums[source, pl.ds(share * d + s * STRIP, height), :]
                if s < 3:
                    strip = pltpu.roll(rest, 96 - 32 * s, 1)
                else:
                    strip = jnp.zeros((STRIP, cols), F32)
                mixed = jnp.where(lane[:height] < channels, main, strip[:height])
                target[d, pl.ds(s * STRIP, height), :] = mixed * scale


def branch_kernel(flags, x, act, a_far, side, w_two, block_out, pa):
    frames, rows, channels, cols = x.shape
    fill(pa, act, a_far, side, 0, False, flags[0] == 0, lambda v: v)
    for f in range(frames // 2):

        @pl.loop(0, rows, unroll=True)
        def _(r):
            branch = conv_pair(w_two, pa, f, r)
            for half in range(2):
                part = slice(half * cols, (half + 1) * cols)
                at = f + 2 * half
                block_out[at, r] = x[at, r].astype(F32) + branch[:, part]


def input_kernel(flags, x, c, grad, g_far, side, w_one_back, input_out, pg):
    frames, rows, channels, cols = x.shape
    fill(pg, grad, g_far, side, frames, True, flags[0] == 0, lambda v: v)
    for f in range(frames // 2):

        @pl.loop(0, rows, unroll=True)
        def _(r):
            back = conv_pair(w_one_back, pg, f, r)
            for half in range(2):
                part = slice(half * cols, (half + 1) * cols)
                at = f + 2 * half
                _, grad_in = norm_silu_and_grad(x[at, r].astype(F32), back[:, part])
                input_out[at, r] = c[at, r].astype(F32) + grad_in


def weights_kernel(first, second, w_one, w_two_back, w_two, w_one_back):
    channels = first.shape[0]
    for source, ahead, back in ((first, w_one, w_one_back), (second, w_two, w_two_back)):
        whole = source[...].astype(F32)
        taps = [whole[:, t * channels : (t + 1) * channels] for t in range(27)]
        for kw in range(3):
            rows = pl.ds(kw * channels, channels)
            ahead[rows, :] = jnp.concatenate([taps[3 * k + kw] for k in range(9)], axis=1).astype(BF16)
            back[rows, :] = jnp.concatenate([taps[26 - 3 * k - kw].T for k in range(9)], axis=1).astype(BF16)


def weights(first, second):
    turned = jax.ShapeDtypeStruct((3 * first.shape[0], first.shape[1] // 3), BF16)
    vmem = pl.BlockSpec(memory_space=pltpu.VMEM)
    return pl.pallas_call(
        weights_kernel,
        out_shape=(turned,) * 4,
        in_specs=[vmem] * 2,
        out_specs=[vmem] * 4,
        compiler_params=pltpu.CompilerParams(vmem_limit_bytes=10 * 1024 * 1024),
        cost_estimate=pl.CostEstimate(flops=3 * 10**9, bytes_accessed=6 * first.size, transcendentals=0),
    )(first, second)


def call(kernel, outs, scratch, flops, args, mib=12):
    vmem = pl.BlockSpec(memory_space=pltpu.VMEM)
    moved = sum(a.size * a.dtype.itemsize for a in list(args[1:]) + list(outs))
    return pl.pallas_call(
        kernel,
        out_shape=outs,
        in_specs=[pl.BlockSpec(memory_space=pltpu.SMEM)] + [vmem] * (len(args) - 1),
        out_specs=[vmem] * len(outs),
        scratch_shapes=scratch,
        compiler_params=pltpu.CompilerParams(vmem_limit_bytes=mib * 1024 * 1024),
        cost_estimate=pl.CostEstimate(flops=flops, bytes_accessed=moved, transcendentals=0),
    )(*args)


def from_before(field, edge):
    frames = field.shape[0]
    sent = jnp.concatenate([field[frames - 2 :], edge[frames - 2 : frames, None]], axis=1)
    return lax.ppermute(sent, TIME, [(i, i + 1) for i in range(lax.axis_size(TIME) - 1)])


def ahead_of(field, edge):
    frames = field.shape[0]
    return jnp.concatenate([field[:2], edge[frames : frames + 2, None]], axis=1)


def from_after(sent):
    return lax.ppermute(sent, TIME, [(i + 1, i) for i in range(lax.axis_size(TIME) - 1)])


def chip_total(kept, given):
    return (kept + lax.ppermute(given, "core", SWAP)).astype(BF16)


def clip_total(pieces):
    arrived = lax.all_to_all(pieces, CLIP_AXES, 0, 0, tiled=True)
    total = jax.ShapeDtypeStruct(pieces.shape[1:], F32)
    return small_call(total_kernel, (total,), (arrived,), False)[0]


def exchanged(parts):
    return lax.all_to_all(parts, "z", 0, 0, tiled=True)


def total_kernel(arrived, total):
    acc = arrived[0].astype(F32)
    for d in range(1, arrived.shape[0]):
        acc = acc + arrived[d].astype(F32)
    total[...] = acc


def spread_kernel(mine, other, sent):
    value = mine[...] + other[...]
    for d in range(sent.shape[0]):
        sent[d] = value


def unpack_kernel(flags, whole, other, first, second):
    channels, share = first.shape
    left = share - MAIN
    cols = whole.shape[1]

    def write(target, packed):
        target[:, pl.ds(0, MAIN)] = packed[...].T[:channels]
        lane = lax.broadcasted_iota(jnp.int32, (STRIP, cols), 1)
        width = cols - channels
        strips = [pltpu.roll(packed[pl.ds(s * STRIP, STRIP), :], (s + 1) * width, 1) for s in range(3)]
        rest = jnp.where(lane < width, strips[0], jnp.where(lane < 2 * width, strips[1], strips[2]))
        target[:, pl.ds(MAIN, left)] = rest.T[:channels, :left]

    for core, pair in ((0, (first, second)), (1, (second, first))):

        @pl.when(flags[1] == core)
        def _():
            write(pair[0], whole)
            write(pair[1], other)


def small_call(kernel, outs, args, flagged):
    vmem = pl.BlockSpec(memory_space=pltpu.VMEM)
    moved = sum(a.size * a.dtype.itemsize for a in list(args) + list(outs))
    specs = [vmem] * len(args)
    if flagged:
        specs[0] = pl.BlockSpec(memory_space=pltpu.SMEM)
    return pl.pallas_call(
        kernel,
        out_shape=outs,
        in_specs=specs,
        out_specs=[vmem] * len(outs),
        compiler_params=pltpu.CompilerParams(vmem_limit_bytes=4 * 1024 * 1024),
        cost_estimate=pl.CostEstimate(flops=0, bytes_accessed=moved, transcendentals=0),
    )(*args)


def head(source, x_far, upstream, c_far, side, w_one, w_two_back, flags, owners, scale):
    frames, rows, channels, cols = source.shape
    field = jax.ShapeDtypeStruct(source.shape, BF16)
    packed = jax.ShapeDtypeStruct((owners, MAIN, cols), F32)
    pairs = pltpu.VMEM((frames, rows + 2, channels, 2 * cols), BF16)
    spots = frames * rows // 2
    conv_flops = 2 * 27 * channels * channels * frames * rows * cols
    return call(
        functools.partial(head_kernel, scale, owners),
        (field, field, jax.ShapeDtypeStruct((2 * frames, channels, cols), BF16), packed, packed),
        [
            pairs,
            pairs,
            pltpu.VMEM((spots, 3 * channels, 2 * cols), BF16),
            pltpu.VMEM((spots, 3 * channels, 2 * cols), BF16),
            pltpu.VMEM((2, 27 * channels + 32, cols), F32),
        ],
        4 * conv_flops,
        (flags, source, x_far, upstream, c_far, side, w_one, w_two_back),
        mib=22,
    )


def local(clip_input, cotangent, first_kernel, second_kernel):
    source, upstream = clip_input[0], cotangent[0]
    frames, rows, channels, cols = source.shape
    half, core = lax.axis_index("x_hi"), lax.axis_index("core")
    flags = jnp.stack([half, core]).astype(jnp.int32)
    edge = jnp.where(half == 0, rows - 1, 0)
    side = jnp.concatenate(
        [lax.dynamic_index_in_dim(a, edge, 1, keepdims=False) for a in (source, upstream)], axis=0
    )
    w_one, w_two_back, w_two, w_one_back = weights(first_kernel.T, second_kernel.T)
    side = lax.ppermute(side, "x_hi", SWAP)
    x_far = from_before(source, side)
    c_far = from_after(ahead_of(upstream, side))

    owners = lax.axis_size(CLIP_AXES)
    positions = frames * rows * cols * lax.axis_size(CLIP_AXES + HALVES)
    act, grad, side, kept, given = head(
        source, x_far, upstream, c_far, side, w_one, w_two_back, flags, owners, 1.0 / math.sqrt(positions)
    )
    pairs = pltpu.VMEM((frames, rows + 2, channels, 2 * cols), BF16)
    conv_flops = 2 * 27 * channels * channels * frames * rows * cols
    out = jax.ShapeDtypeStruct(source.shape, F32)
    peers = lax.axis_size("z")
    part_shape = (MAIN // peers, cols)

    pieces, side = lax.optimization_barrier((chip_total(kept, given), side))
    clip_sum = clip_total(pieces)
    side = lax.ppermute(side, "x_hi", SWAP)
    a_far = from_before(act, side)
    clip_sum, g_sent = lax.optimization_barrier((clip_sum, ahead_of(grad, side)))
    parts = exchanged(clip_sum.reshape((peers,) + part_shape))
    g_far = from_after(g_sent)
    part = jax.ShapeDtypeStruct(part_shape, F32)
    (part_sum,) = small_call(total_kernel, (part,), (parts,), False)
    part_sum, a_far = lax.optimization_barrier((part_sum, a_far))
    part_other = lax.ppermute(part_sum, "x_hi", SWAP)
    (block_output,) = call(
        branch_kernel, (out,), [pairs], conv_flops, (flags, source, act, a_far, side, w_two)
    )
    part_other, block_output = lax.optimization_barrier((part_other, block_output))
    spread = jax.ShapeDtypeStruct((peers,) + part_shape, F32)
    (sent,) = small_call(spread_kernel, (spread,), (part_sum, part_other), False)
    sent, g_far = lax.optimization_barrier((sent, g_far))
    whole = exchanged(sent).reshape(MAIN, -1)
    (input_grad,) = call(
        input_kernel, (out,), [pairs], conv_flops, (flags, source, upstream, grad, g_far, side, w_one_back)
    )
    whole, input_grad = lax.optimization_barrier((whole, input_grad))
    other = lax.ppermute(whole, "core", SWAP)
    owned = jax.ShapeDtypeStruct((channels, 27 * channels // owners), F32)
    first_grad, second_grad = small_call(unpack_kernel, (owned, owned), (flags, whole, other), True)
    return (
        block_output[None],
        input_grad[None],
        first_grad.T,
        second_grad.T,
    )


def solution(mesh):
    shape = mesh.shape
    axes = CLIP_AXES + TIME + ("x_hi",)
    split = Mesh(mesh.devices.reshape(2, shape["dp"] // 2, shape["tm"] // 2, 2, shape["height"]), axes)
    field = P(CLIP_AXES, TIME, "x_hi", None, None)
    return jax.shard_map(
        local,
        mesh=split,
        in_specs=(field, field, P(), P()),
        out_specs=(field, field, P(CLIP_AXES, None), P(CLIP_AXES, None)),
        check_vma=False,
    )
```

```python
import functools
import math

import jax
import jax.numpy as jnp
from jax import lax
from jax.experimental import pallas as pl
from jax.experimental.pallas import tpu as pltpu
from jax.sharding import Mesh, PartitionSpec as P

EPSILON = 1e-06
TIME = ("z", "core")
CLIP_AXES = ("x_lo", "y")
HALVES = ("z", "core", "x_hi")
SWAP = [(0, 1), (1, 0)]
BF16, F32 = jnp.bfloat16, jnp.float32

MAIN, STRIP = 256, 80


def sigmoid(u):
    return 0.5 + 0.5 * jnp.tanh(0.5 * u)


def normed(v):
    scale = lax.rsqrt(jnp.mean(v * v, axis=0, keepdims=True) + EPSILON)
    return v * scale, scale


def norm_silu(v):
    u, _ = normed(v)
    return u * sigmoid(u)


def norm_silu_and_grad(v, back):
    u, scale = normed(v)
    gate = sigmoid(u)
    inner = back * (gate * (1.0 + u * (1.0 - gate)))
    grad = scale * (inner - u * jnp.mean(u * inner, axis=0, keepdims=True))
    return u * gate, grad


def fill(pairs, own, far, side, side_at, own_first, is_upper, change):
    frames, extra, rows, cols = own.shape[0], far.shape[0], own.shape[1], own.shape[3]
    upper = is_upper.astype(F32)
    own_at, far_at = (0, frames) if own_first else (extra, 0)

    def put(value, frame, row):
        value = value.astype(BF16)
        if frame < frames:
            pairs[frame, row, :, pl.ds(0, cols)] = value
        if frame >= 2:
            pairs[frame - 2, row, :, pl.ds(cols, cols)] = value

    for field, base in ((own, own_at), (far, far_at)):
        for f in range(field.shape[0]):
            for r in range(rows):
                put(change(field[f, r].astype(F32)), base + f, r + 1)
            edge = side[side_at + f] if field is own else far[f, rows]
            value = change(edge.astype(F32))
            put(value * (1.0 - upper), base + f, 0)
            put(value * upper, base + f, rows + 1)


def shifted(value, by):
    cols = value.shape[1]
    lane = lax.broadcasted_iota(jnp.int32, value.shape, 1)
    return jnp.where(lane == (0 if by == 1 else cols - 1), 0.0, pltpu.roll(value, by % cols, 1))


def halves(value):
    cols = value.shape[1] // 2
    return value[:, :cols], value[:, cols:]


def conv_pair(weight, pairs, f, r):
    channels = pairs.shape[2]
    stacked = jnp.concatenate(
        [pairs[f + kt, pl.ds(r, 3)].reshape(3 * channels, -1) for kt in range(3)], axis=0
    )
    product = jnp.dot(weight[...], stacked, preferred_element_type=F32)
    return jnp.concatenate(
        [
            shifted(part[:channels], 1) + part[channels : 2 * channels] + shifted(part[2 * channels :], -1)
            for part in halves(product)
        ],
        axis=1,
    )


def put_shifts(target, spot, value):
    channels = value.shape[0]
    cols = value.shape[1] // 2
    for half, part in enumerate(halves(value)):
        lanes = pl.ds(half * cols, cols)
        for k, by in ((0, -1), (1, 0), (2, 1)):
            moved = shifted(part, by) if by else part
            target[spot, pl.ds(k * channels, channels), lanes] = moved.astype(BF16)


def nt_dot(left, right):
    return lax.dot_general(left, right, (((1,), (1,)), ((), ())), preferred_element_type=F32)


def head_kernel(
    scale, owners, flags, x, x_far, c, c_far, side, w_one, w_two_back,
    act_out, grad_out, side_out, kept, given, px, pc, lanes_act, lanes_grad, sums,
):
    frames, rows, channels, cols = x.shape
    is_upper, core = flags[0] == 0, flags[1]
    fill(px, x, x_far, side, 0, False, is_upper, norm_silu)
    fill(pc, c, c_far, side, frames, True, is_upper, lambda v: v)

    for f in range(frames // 2):

        @pl.loop(0, rows, unroll=True)
        def _(r):
            middle = conv_pair(w_one, px, f, r)
            back = conv_pair(w_two_back, pc, f, r)
            act, grad = norm_silu_and_grad(middle, back)
            spot = f * rows + r
            put_shifts(lanes_act, spot, act)
            put_shifts(lanes_grad, spot, grad)
            for half in range(2):
                act_out[f + 2 * half, r] = act[:, half * cols : (half + 1) * cols].astype(BF16)
                grad_out[f + 2 * half, r] = grad[:, half * cols : (half + 1) * cols].astype(BF16)

    edge = jnp.where(is_upper, rows - 1, 0)
    for f in range(frames):
        side_out[f] = act_out[f, edge]
        side_out[frames + f] = grad_out[f, edge]

    spots = [(f, r) for f in range(frames // 2) for r in range(rows)]
    taps = 3 * channels

    def lined(scratch):
        return jnp.concatenate([scratch[i] for i in range(len(spots))], axis=1)

    def padded(pairs, kt):
        return jnp.concatenate([pairs[f + kt, pl.ds(r, 3)].reshape(taps, -1) for f, r in spots], axis=1)

    @pl.loop(0, 3, unroll=True)
    def _(kt):
        product = nt_dot(padded(px, kt), lined(lanes_grad))
        for kh in range(3):
            for kw in range(3):
                first = pl.multiple_of((9 * kt + 3 * kh + kw) * channels, 8)
                block = product[kh * channels : (kh + 1) * channels, kw * channels : (kw + 1) * channels]
                sums[0, pl.ds(first, channels), pl.ds(0, channels)] = block

    @pl.loop(0, 3, unroll=True)
    def _(kt):
        product = nt_dot(lined(lanes_act), padded(pc, kt))
        for kh in range(3):
            for kw in range(3):
                first = pl.multiple_of((26 - (9 * kt + 3 * kh + kw)) * channels, 8)
                block = product[kw * channels : (kw + 1) * channels, kh * channels : (kh + 1) * channels]
                sums[1, pl.ds(first, channels), pl.ds(0, channels)] = block

    total = 27 * channels
    sums[:, pl.ds(total, sums.shape[1] - total), :] = jnp.zeros((2, sums.shape[1] - total, cols), F32)
    share = total // owners
    lane = lax.broadcasted_iota(jnp.int32, (STRIP, cols), 1)
    for target, source in ((kept, core), (given, 1 - core)):
        for d in range(owners):
            rest = sums[source, pl.ds(share * d + MAIN, STRIP), :]
            for s in range(4):
                height = min(STRIP, MAIN - s * STRIP)
                main = sums[source, pl.ds(share * d + s * STRIP, height), :]
                if s < 3:
                    strip = pltpu.roll(rest, 96 - 32 * s, 1)
                else:
                    strip = jnp.zeros((STRIP, cols), F32)
                mixed = jnp.where(lane[:height] < channels, main, strip[:height])
                target[d, pl.ds(s * STRIP, height), :] = (mixed * scale).astype(target.dtype)


def branch_kernel(flags, x, act, a_far, side, k_two, block_out, pa, w_two):
    frames, rows, channels, cols = x.shape
    lay_forward(k_two, w_two)
    fill(pa, act, a_far, side, 0, False, flags[0] == 0, lambda v: v)
    for f in range(frames // 2):

        @pl.loop(0, rows, unroll=True)
        def _(r):
            branch = conv_pair(w_two, pa, f, r)
            for half in range(2):
                part = slice(half * cols, (half + 1) * cols)
                at = f + 2 * half
                block_out[at, r] = x[at, r].astype(F32) + branch[:, part]


def input_kernel(flags, x, c, grad, g_far, side, w_one_back, input_out, pg):
    frames, rows, channels, cols = x.shape
    fill(pg, grad, g_far, side, frames, True, flags[0] == 0, lambda v: v)
    for f in range(frames // 2):

        @pl.loop(0, rows, unroll=True)
        def _(r):
            back = conv_pair(w_one_back, pg, f, r)
            for half in range(2):
                part = slice(half * cols, (half + 1) * cols)
                at = f + 2 * half
                _, grad_in = norm_silu_and_grad(x[at, r].astype(F32), back[:, part])
                input_out[at, r] = c[at, r].astype(F32) + grad_in


def lay_forward(kernel, laid):
    channels = kernel.shape[0]
    whole = kernel[...].astype(F32)
    taps = [whole[:, t * channels : (t + 1) * channels] for t in range(27)]
    for kw in range(3):
        row = jnp.concatenate([taps[3 * k + kw] for k in range(9)], axis=1)
        laid[pl.ds(kw * channels, channels), :] = row.astype(BF16)


def lay_backward(kernel, laid):
    channels = kernel.shape[0]
    whole = kernel[...].astype(F32)
    taps = [whole[:, t * channels : (t + 1) * channels] for t in range(27)]
    for kw in range(3):
        row = jnp.concatenate([taps[26 - 3 * k - kw].T for k in range(9)], axis=1)
        laid[pl.ds(kw * channels, channels), :] = row.astype(BF16)


def weights_kernel(first, second, w_one, w_two_back, w_one_back):
    lay_forward(first, w_one)
    lay_backward(second, w_two_back)
    lay_backward(first, w_one_back)


def weights(first, second):
    turned = jax.ShapeDtypeStruct((3 * first.shape[0], first.shape[1] // 3), BF16)
    vmem = pl.BlockSpec(memory_space=pltpu.VMEM)
    return pl.pallas_call(
        weights_kernel,
        out_shape=(turned,) * 3,
        in_specs=[vmem] * 2,
        out_specs=[vmem] * 3,
        compiler_params=pltpu.CompilerParams(vmem_limit_bytes=10 * 1024 * 1024),
        cost_estimate=pl.CostEstimate(flops=3 * 10**9, bytes_accessed=6 * first.size, transcendentals=0),
    )(first, second)


def call(kernel, outs, scratch, flops, args, mib=12):
    vmem = pl.BlockSpec(memory_space=pltpu.VMEM)
    moved = sum(a.size * a.dtype.itemsize for a in list(args[1:]) + list(outs))
    return pl.pallas_call(
        kernel,
        out_shape=outs,
        in_specs=[pl.BlockSpec(memory_space=pltpu.SMEM)] + [vmem] * (len(args) - 1),
        out_specs=[vmem] * len(outs),
        scratch_shapes=scratch,
        compiler_params=pltpu.CompilerParams(vmem_limit_bytes=mib * 1024 * 1024),
        cost_estimate=pl.CostEstimate(flops=flops, bytes_accessed=moved, transcendentals=0),
    )(*args)


def join_kernel(earlier, later, side, last, first):
    frames, rows = earlier.shape[0], earlier.shape[1]
    for f in range(2):
        last[f, pl.ds(0, rows)] = earlier[frames - 2 + f]
        last[f, rows] = side[frames - 2 + f]
        first[f, pl.ds(0, rows)] = later[f]
        first[f, rows] = side[frames + f]


def joined(earlier, later, side):
    _, rows, channels, cols = earlier.shape
    out = jax.ShapeDtypeStruct((2, rows + 1, channels, cols), BF16)
    return small_call(join_kernel, (out, out), (earlier, later, side), False)


def from_before(sent):
    return lax.ppermute(sent, TIME, [(i, i + 1) for i in range(lax.axis_size(TIME) - 1)])


def from_after(sent):
    return lax.ppermute(sent, TIME, [(i + 1, i) for i in range(lax.axis_size(TIME) - 1)])


def chip_total(kept, given):
    return (kept + lax.ppermute(given, "core", SWAP).astype(F32)).astype(BF16)


def clip_total(pieces):
    arrived = lax.all_to_all(pieces, CLIP_AXES, 0, 0, tiled=True)
    total = jax.ShapeDtypeStruct(pieces.shape[1:], F32)
    return small_call(total_kernel, (total,), (arrived,), False)[0]


def exchanged(parts):
    return lax.all_to_all(parts, "z", 0, 0, tiled=True)


def total_kernel(arrived, total):
    acc = arrived[0].astype(F32)
    for d in range(1, arrived.shape[0]):
        acc = acc + arrived[d].astype(F32)
    total[...] = acc


def spread_kernel(mine, other, sent):
    value = mine[...] + other[...]
    for d in range(sent.shape[0]):
        sent[d] = value


def unpack_kernel(flags, whole, other, first, second):
    channels, share = first.shape
    left = share - MAIN
    cols = whole.shape[1]

    def write(target, packed):
        target[:, pl.ds(0, MAIN)] = packed[...].T[:channels]
        lane = lax.broadcasted_iota(jnp.int32, (STRIP, cols), 1)
        width = cols - channels
        strips = [pltpu.roll(packed[pl.ds(s * STRIP, STRIP), :], (s + 1) * width, 1) for s in range(3)]
        rest = jnp.where(lane < width, strips[0], jnp.where(lane < 2 * width, strips[1], strips[2]))
        target[:, pl.ds(MAIN, left)] = rest.T[:channels, :left]

    for core, pair in ((0, (first, second)), (1, (second, first))):

        @pl.when(flags[1] == core)
        def _():
            write(pair[0], whole)
            write(pair[1], other)


def small_call(kernel, outs, args, flagged):
    vmem = pl.BlockSpec(memory_space=pltpu.VMEM)
    moved = sum(a.size * a.dtype.itemsize for a in list(args) + list(outs))
    specs = [vmem] * len(args)
    if flagged:
        specs[0] = pl.BlockSpec(memory_space=pltpu.SMEM)
    return pl.pallas_call(
        kernel,
        out_shape=outs,
        in_specs=specs,
        out_specs=[vmem] * len(outs),
        compiler_params=pltpu.CompilerParams(vmem_limit_bytes=4 * 1024 * 1024),
        cost_estimate=pl.CostEstimate(flops=0, bytes_accessed=moved, transcendentals=0),
    )(*args)


def head(source, x_far, upstream, c_far, side, w_one, w_two_back, flags, owners, scale):
    frames, rows, channels, cols = source.shape
    field = jax.ShapeDtypeStruct(source.shape, BF16)
    packed = jax.ShapeDtypeStruct((owners, MAIN, cols), F32)
    pairs = pltpu.VMEM((frames, rows + 2, channels, 2 * cols), BF16)
    spots = frames * rows // 2
    conv_flops = 2 * 27 * channels * channels * frames * rows * cols
    return call(
        functools.partial(head_kernel, scale, owners),
        (field, field, jax.ShapeDtypeStruct((2 * frames, channels, cols), BF16), packed, jax.ShapeDtypeStruct(packed.shape, BF16)),
        [
            pairs,
            pairs,
            pltpu.VMEM((spots, 3 * channels, 2 * cols), BF16),
            pltpu.VMEM((spots, 3 * channels, 2 * cols), BF16),
            pltpu.VMEM((2, 27 * channels + 32, cols), F32),
        ],
        4 * conv_flops,
        (flags, source, x_far, upstream, c_far, side, w_one, w_two_back),
        mib=22,
    )


def local(clip_input, cotangent, first_kernel, second_kernel):
    source, upstream = clip_input[0], cotangent[0]
    frames, rows, channels, cols = source.shape
    half, core = lax.axis_index("x_hi"), lax.axis_index("core")
    flags = jnp.stack([half, core]).astype(jnp.int32)
    edge = jnp.where(half == 0, rows - 1, 0)
    side = jnp.concatenate(
        [lax.dynamic_index_in_dim(a, edge, 1, keepdims=False) for a in (source, upstream)], axis=0
    )
    w_one, w_two_back, w_one_back = weights(first_kernel.T, second_kernel.T)
    side = lax.ppermute(side, "x_hi", SWAP)
    x_sent, c_sent = joined(source, upstream, side)
    x_far, c_far = from_before(x_sent), from_after(c_sent)

    owners = lax.axis_size(CLIP_AXES)
    positions = frames * rows * cols * lax.axis_size(CLIP_AXES + HALVES)
    act, grad, side, kept, given = head(
        source, x_far, upstream, c_far, side, w_one, w_two_back, flags, owners, 1.0 / math.sqrt(positions)
    )
    pairs = pltpu.VMEM((frames, rows + 2, channels, 2 * cols), BF16)
    conv_flops = 2 * 27 * channels * channels * frames * rows * cols
    out = jax.ShapeDtypeStruct(source.shape, F32)
    laid = pltpu.VMEM((3 * channels, 9 * channels), BF16)
    peers = lax.axis_size("z")
    part_shape = (MAIN // peers, cols)

    pieces, side = lax.optimization_barrier((chip_total(kept, given), side))
    clip_sum = clip_total(pieces)
    side = lax.ppermute(side, "x_hi", SWAP)
    a_sent, g_sent = joined(act, grad, side)
    a_far = from_before(a_sent)
    clip_sum, g_sent = lax.optimization_barrier((clip_sum, g_sent))
    parts = exchanged(clip_sum.reshape((peers,) + part_shape))
    g_far = from_after(g_sent)
    part = jax.ShapeDtypeStruct(part_shape, F32)
    (part_sum,) = small_call(total_kernel, (part,), (parts,), False)
    part_sum, a_far = lax.optimization_barrier((part_sum, a_far))
    part_other = lax.ppermute(part_sum, "x_hi", SWAP)
    (block_output,) = call(
        branch_kernel, (out,), [pairs, laid], conv_flops, (flags, source, act, a_far, side, second_kernel.T)
    )
    part_other, block_output = lax.optimization_barrier((part_other, block_output))
    spread = jax.ShapeDtypeStruct((peers,) + part_shape, F32)
    (sent,) = small_call(spread_kernel, (spread,), (part_sum, part_other), False)
    sent, g_far = lax.optimization_barrier((sent, g_far))
    whole = exchanged(sent).reshape(MAIN, -1)
    (input_grad,) = call(
        input_kernel, (out,), [pairs], conv_flops, (flags, source, upstream, grad, g_far, side, w_one_back)
    )
    whole, input_grad = lax.optimization_barrier((whole, input_grad))
    other = lax.ppermute(whole, "core", SWAP)
    owned = jax.ShapeDtypeStruct((channels, 27 * channels // owners), F32)
    first_grad, second_grad = small_call(unpack_kernel, (owned, owned), (flags, whole, other), True)
    return (
        block_output[None],
        input_grad[None],
        first_grad.T,
        second_grad.T,
    )


def solution(mesh):
    shape = mesh.shape
    axes = CLIP_AXES + TIME + ("x_hi",)
    split = Mesh(mesh.devices.reshape(2, shape["dp"] // 2, shape["tm"] // 2, 2, shape["height"]), axes)
    field = P(CLIP_AXES, TIME, "x_hi", None, None)
    return jax.shard_map(
        local,
        mesh=split,
        in_specs=(field, field, P(), P()),
        out_specs=(field, field, P(CLIP_AXES, None), P(CLIP_AXES, None)),
        check_vma=False,
    )
```

```python
import functools
import math

import jax
import jax.numpy as jnp
from jax import lax
from jax.experimental import pallas as pl
from jax.experimental.pallas import tpu as pltpu
from jax.sharding import Mesh, PartitionSpec as P

EPSILON = 1e-06
TIME = ("z", "core")
CLIP_AXES = ("x_lo", "y")
HALVES = ("z", "core", "x_hi")
SWAP = [(0, 1), (1, 0)]
BF16, F32 = jnp.bfloat16, jnp.float32

MAIN, STRIP = 256, 80


def sigmoid(u):
    return 0.5 + 0.5 * jnp.tanh(0.5 * u)


def normed(v):
    scale = lax.rsqrt(jnp.mean(v * v, axis=0, keepdims=True) + EPSILON)
    return v * scale, scale


def norm_silu(v):
    u, _ = normed(v)
    return u * sigmoid(u)


def norm_silu_and_grad(v, back):
    u, scale = normed(v)
    gate = sigmoid(u)
    inner = back * (gate * (1.0 + u * (1.0 - gate)))
    grad = scale * (inner - u * jnp.mean(u * inner, axis=0, keepdims=True))
    return u * gate, grad


def fill(pairs, own, far, side, side_at, own_first, is_upper, change):
    frames, extra, rows, cols = own.shape[0], far.shape[0], own.shape[1], own.shape[3]
    upper = is_upper.astype(F32)
    own_at, far_at = (0, frames) if own_first else (extra, 0)

    def put(value, frame, row):
        value = value.astype(BF16)
        if frame < frames:
            pairs[frame, row, :, pl.ds(0, cols)] = value
        if frame >= 2:
            pairs[frame - 2, row, :, pl.ds(cols, cols)] = value

    for field, base in ((own, own_at), (far, far_at)):
        for f in range(field.shape[0]):
            for r in range(rows):
                put(change(field[f, r].astype(F32)), base + f, r + 1)
            edge = side[side_at + f] if field is own else far[f, rows]
            value = change(edge.astype(F32))
            put(value * (1.0 - upper), base + f, 0)
            put(value * upper, base + f, rows + 1)


def shifted(value, by):
    cols = value.shape[1]
    lane = lax.broadcasted_iota(jnp.int32, value.shape, 1)
    return jnp.where(lane == (0 if by == 1 else cols - 1), 0.0, pltpu.roll(value, by % cols, 1))


def halves(value):
    cols = value.shape[1] // 2
    return value[:, :cols], value[:, cols:]


def conv_pair(weight, pairs, f, r):
    channels = pairs.shape[2]
    stacked = jnp.concatenate(
        [pairs[f + kt, pl.ds(r, 3)].reshape(3 * channels, -1) for kt in range(3)], axis=0
    )
    product = jnp.dot(weight[...], stacked, preferred_element_type=F32)
    return jnp.concatenate(
        [
            shifted(part[:channels], 1) + part[channels : 2 * channels] + shifted(part[2 * channels :], -1)
            for part in halves(product)
        ],
        axis=1,
    )


def put_shifts(target, spot, value):
    channels = value.shape[0]
    cols = value.shape[1] // 2
    for half, part in enumerate(halves(value)):
        lanes = pl.ds(half * cols, cols)
        for k, by in ((0, -1), (1, 0), (2, 1)):
            moved = shifted(part, by) if by else part
            target[spot, pl.ds(k * channels, channels), lanes] = moved.astype(BF16)


def nt_dot(left, right):
    return lax.dot_general(left, right, (((1,), (1,)), ((), ())), preferred_element_type=F32)


def head_kernel(
    scale, owners, flags, x, x_far, c, c_far, side, w_one, w_two_back,
    act_out, grad_out, side_out, kept, given, px, pc, lanes_act, lanes_grad, sums,
):
    frames, rows, channels, cols = x.shape
    is_upper, core = flags[0] == 0, flags[1]
    fill(px, x, x_far, side, 0, False, is_upper, norm_silu)
    fill(pc, c, c_far, side, frames, True, is_upper, lambda v: v)

    for f in range(frames // 2):

        @pl.loop(0, rows, unroll=True)
        def _(r):
            middle = conv_pair(w_one, px, f, r)
            back = conv_pair(w_two_back, pc, f, r)
            act, grad = norm_silu_and_grad(middle, back)
            spot = f * rows + r
            put_shifts(lanes_act, spot, act)
            put_shifts(lanes_grad, spot, grad)
            for half in range(2):
                act_out[f + 2 * half, r] = act[:, half * cols : (half + 1) * cols].astype(BF16)
                grad_out[f + 2 * half, r] = grad[:, half * cols : (half + 1) * cols].astype(BF16)

    edge = jnp.where(is_upper, rows - 1, 0)
    for f in range(frames):
        side_out[f] = act_out[f, edge]
        side_out[frames + f] = grad_out[f, edge]

    spots = [(f, r) for f in range(frames // 2) for r in range(rows)]
    taps = 3 * channels

    def lined(scratch):
        return jnp.concatenate([scratch[i] for i in range(len(spots))], axis=1)

    def padded(pairs, kt):
        return jnp.concatenate([pairs[f + kt, pl.ds(r, 3)].reshape(taps, -1) for f, r in spots], axis=1)

    @pl.loop(0, 3, unroll=True)
    def _(kt):
        product = nt_dot(padded(px, kt), lined(lanes_grad))
        for kh in range(3):
            for kw in range(3):
                first = pl.multiple_of((9 * kt + 3 * kh + kw) * channels, 8)
                block = product[kh * channels : (kh + 1) * channels, kw * channels : (kw + 1) * channels]
                sums[0, pl.ds(first, channels), pl.ds(0, channels)] = block

    @pl.loop(0, 3, unroll=True)
    def _(kt):
        product = nt_dot(lined(lanes_act), padded(pc, kt))
        for kh in range(3):
            for kw in range(3):
                first = pl.multiple_of((26 - (9 * kt + 3 * kh + kw)) * channels, 8)
                block = product[kw * channels : (kw + 1) * channels, kh * channels : (kh + 1) * channels]
                sums[1, pl.ds(first, channels), pl.ds(0, channels)] = block

    total = 27 * channels
    sums[:, pl.ds(total, sums.shape[1] - total), :] = jnp.zeros((2, sums.shape[1] - total, cols), F32)
    share = total // owners
    lane = lax.broadcasted_iota(jnp.int32, (STRIP, cols), 1)
    for target, source in ((kept, core), (given, 1 - core)):
        for d in range(owners):
            rest = sums[source, pl.ds(share * d + MAIN, STRIP), :]
            for s in range(4):
                height = min(STRIP, MAIN - s * STRIP)
                main = sums[source, pl.ds(share * d + s * STRIP, height), :]
                if s < 3:
                    strip = pltpu.roll(rest, 96 - 32 * s, 1)
                else:
                    strip = jnp.zeros((STRIP, cols), F32)
                mixed = jnp.where(lane[:height] < channels, main, strip[:height])
                target[d, pl.ds(s * STRIP, height), :] = (mixed * scale).astype(target.dtype)


def branch_kernel(flags, x, act, a_far, side, k_two, block_out, pa, w_two):
    frames, rows, channels, cols = x.shape
    lay_forward(k_two, w_two)
    fill(pa, act, a_far, side, 0, False, flags[0] == 0, lambda v: v)
    for f in range(frames // 2):

        @pl.loop(0, rows, unroll=True)
        def _(r):
            branch = conv_pair(w_two, pa, f, r)
            for half in range(2):
                part = slice(half * cols, (half + 1) * cols)
                at = f + 2 * half
                block_out[at, r] = x[at, r].astype(F32) + branch[:, part]


def input_kernel(flags, x, c, grad, g_far, side, w_one_back, input_out, pg):
    frames, rows, channels, cols = x.shape
    fill(pg, grad, g_far, side, frames, True, flags[0] == 0, lambda v: v)
    for f in range(frames // 2):

        @pl.loop(0, rows, unroll=True)
        def _(r):
            back = conv_pair(w_one_back, pg, f, r)
            for half in range(2):
                part = slice(half * cols, (half + 1) * cols)
                at = f + 2 * half
                _, grad_in = norm_silu_and_grad(x[at, r].astype(F32), back[:, part])
                input_out[at, r] = c[at, r].astype(F32) + grad_in


def lay_forward(kernel, laid):
    channels = kernel.shape[0]
    whole = kernel[...].astype(F32)
    taps = [whole[:, t * channels : (t + 1) * channels] for t in range(27)]
    for kw in range(3):
        row = jnp.concatenate([taps[3 * k + kw] for k in range(9)], axis=1)
        laid[pl.ds(kw * channels, channels), :] = row.astype(BF16)


def lay_backward(kernel, laid):
    channels = kernel.shape[0]
    whole = kernel[...].astype(F32)
    taps = [whole[:, t * channels : (t + 1) * channels] for t in range(27)]
    for kw in range(3):
        row = jnp.concatenate([taps[26 - 3 * k - kw].T for k in range(9)], axis=1)
        laid[pl.ds(kw * channels, channels), :] = row.astype(BF16)


def weights_kernel(first, second, w_one, w_two_back, w_one_back):
    lay_forward(first, w_one)
    lay_backward(second, w_two_back)
    lay_backward(first, w_one_back)


def weights(first, second):
    turned = jax.ShapeDtypeStruct((3 * first.shape[0], first.shape[1] // 3), BF16)
    vmem = pl.BlockSpec(memory_space=pltpu.VMEM)
    return pl.pallas_call(
        weights_kernel,
        out_shape=(turned,) * 3,
        in_specs=[vmem] * 2,
        out_specs=[vmem] * 3,
        compiler_params=pltpu.CompilerParams(vmem_limit_bytes=10 * 1024 * 1024),
        cost_estimate=pl.CostEstimate(flops=3 * 10**9, bytes_accessed=6 * first.size, transcendentals=0),
    )(first, second)


def call(kernel, outs, scratch, flops, args, mib=12):
    vmem = pl.BlockSpec(memory_space=pltpu.VMEM)
    moved = sum(a.size * a.dtype.itemsize for a in list(args[1:]) + list(outs))
    return pl.pallas_call(
        kernel,
        out_shape=outs,
        in_specs=[pl.BlockSpec(memory_space=pltpu.SMEM)] + [vmem] * (len(args) - 1),
        out_specs=[vmem] * len(outs),
        scratch_shapes=scratch,
        compiler_params=pltpu.CompilerParams(vmem_limit_bytes=mib * 1024 * 1024),
        cost_estimate=pl.CostEstimate(flops=flops, bytes_accessed=moved, transcendentals=0),
    )(*args)


def from_before(field, edge):
    frames = field.shape[0]
    sent = jnp.concatenate([field[frames - 2 :], edge[frames - 2 : frames, None]], axis=1)
    return lax.ppermute(sent, TIME, [(i, i + 1) for i in range(lax.axis_size(TIME) - 1)])


def ahead_of(field, edge):
    frames = field.shape[0]
    return jnp.concatenate([field[:2], edge[frames : frames + 2, None]], axis=1)


def from_after(sent):
    return lax.ppermute(sent, TIME, [(i + 1, i) for i in range(lax.axis_size(TIME) - 1)])


def chip_total(kept, given):
    return (kept + lax.ppermute(given, "core", SWAP).astype(F32)).astype(BF16)


def clip_total(pieces):
    arrived = lax.all_to_all(pieces, CLIP_AXES, 0, 0, tiled=True)
    total = jax.ShapeDtypeStruct(pieces.shape[1:], F32)
    return small_call(total_kernel, (total,), (arrived,), False)[0]


def exchanged(parts):
    return lax.all_to_all(parts, "z", 0, 0, tiled=True)


def total_kernel(arrived, total):
    acc = arrived[0].astype(F32)
    for d in range(1, arrived.shape[0]):
        acc = acc + arrived[d].astype(F32)
    total[...] = acc


def spread_kernel(mine, other, sent):
    value = mine[...] + other[...]
    for d in range(sent.shape[0]):
        sent[d] = value


def unpack_kernel(flags, whole, other, first, second):
    channels, share = first.shape
    left = share - MAIN
    cols = whole.shape[1]

    def write(target, packed):
        target[:, pl.ds(0, MAIN)] = packed[...].T[:channels]
        lane = lax.broadcasted_iota(jnp.int32, (STRIP, cols), 1)
        width = cols - channels
        strips = [pltpu.roll(packed[pl.ds(s * STRIP, STRIP), :], (s + 1) * width, 1) for s in range(3)]
        rest = jnp.where(lane < width, strips[0], jnp.where(lane < 2 * width, strips[1], strips[2]))
        target[:, pl.ds(MAIN, left)] = rest.T[:channels, :left]

    for core, pair in ((0, (first, second)), (1, (second, first))):

        @pl.when(flags[1] == core)
        def _():
            write(pair[0], whole)
            write(pair[1], other)


def small_call(kernel, outs, args, flagged):
    vmem = pl.BlockSpec(memory_space=pltpu.VMEM)
    moved = sum(a.size * a.dtype.itemsize for a in list(args) + list(outs))
    specs = [vmem] * len(args)
    if flagged:
        specs[0] = pl.BlockSpec(memory_space=pltpu.SMEM)
    return pl.pallas_call(
        kernel,
        out_shape=outs,
        in_specs=specs,
        out_specs=[vmem] * len(outs),
        compiler_params=pltpu.CompilerParams(vmem_limit_bytes=4 * 1024 * 1024),
        cost_estimate=pl.CostEstimate(flops=0, bytes_accessed=moved, transcendentals=0),
    )(*args)


def head(source, x_far, upstream, c_far, side, w_one, w_two_back, flags, owners, scale):
    frames, rows, channels, cols = source.shape
    field = jax.ShapeDtypeStruct(source.shape, BF16)
    packed = jax.ShapeDtypeStruct((owners, MAIN, cols), F32)
    pairs = pltpu.VMEM((frames, rows + 2, channels, 2 * cols), BF16)
    spots = frames * rows // 2
    conv_flops = 2 * 27 * channels * channels * frames * rows * cols
    return call(
        functools.partial(head_kernel, scale, owners),
        (field, field, jax.ShapeDtypeStruct((2 * frames, channels, cols), BF16), packed, jax.ShapeDtypeStruct(packed.shape, BF16)),
        [
            pairs,
            pairs,
            pltpu.VMEM((spots, 3 * channels, 2 * cols), BF16),
            pltpu.VMEM((spots, 3 * channels, 2 * cols), BF16),
            pltpu.VMEM((2, 27 * channels + 32, cols), F32),
        ],
        4 * conv_flops,
        (flags, source, x_far, upstream, c_far, side, w_one, w_two_back),
        mib=22,
    )


def local(clip_input, cotangent, first_kernel, second_kernel):
    source, upstream = clip_input[0], cotangent[0]
    frames, rows, channels, cols = source.shape
    half, core = lax.axis_index("x_hi"), lax.axis_index("core")
    flags = jnp.stack([half, core]).astype(jnp.int32)
    edge = jnp.where(half == 0, rows - 1, 0)
    side = jnp.concatenate(
        [lax.dynamic_index_in_dim(a, edge, 1, keepdims=False) for a in (source, upstream)], axis=0
    )
    w_one, w_two_back, w_one_back = weights(first_kernel.T, second_kernel.T)
    side = lax.ppermute(side, "x_hi", SWAP)
    x_far = from_before(source, side)
    c_far = from_after(ahead_of(upstream, side))

    owners = lax.axis_size(CLIP_AXES)
    positions = frames * rows * cols * lax.axis_size(CLIP_AXES + HALVES)
    act, grad, side, kept, given = head(
        source, x_far, upstream, c_far, side, w_one, w_two_back, flags, owners, 1.0 / math.sqrt(positions)
    )
    pairs = pltpu.VMEM((frames, rows + 2, channels, 2 * cols), BF16)
    conv_flops = 2 * 27 * channels * channels * frames * rows * cols
    out = jax.ShapeDtypeStruct(source.shape, F32)
    laid = pltpu.VMEM((3 * channels, 9 * channels), BF16)
    peers = lax.axis_size("z")
    part_shape = (MAIN // peers, cols)

    pieces, side = lax.optimization_barrier((chip_total(kept, given), side))
    clip_sum = clip_total(pieces)
    side = lax.ppermute(side, "x_hi", SWAP)
    a_far = from_before(act, side)
    clip_sum, g_sent = lax.optimization_barrier((clip_sum, ahead_of(grad, side)))
    parts = exchanged(clip_sum.reshape((peers,) + part_shape))
    g_far = from_after(g_sent)
    part = jax.ShapeDtypeStruct(part_shape, F32)
    (part_sum,) = small_call(total_kernel, (part,), (parts,), False)
    part_sum, a_far = lax.optimization_barrier((part_sum, a_far))
    part_other = lax.ppermute(part_sum, "x_hi", SWAP)
    (block_output,) = call(
        branch_kernel, (out,), [pairs, laid], conv_flops, (flags, source, act, a_far, side, second_kernel.T)
    )
    part_other, block_output = lax.optimization_barrier((part_other, block_output))
    spread = jax.ShapeDtypeStruct((peers,) + part_shape, F32)
    (sent,) = small_call(spread_kernel, (spread,), (part_sum, part_other), False)
    sent, g_far = lax.optimization_barrier((sent, g_far))
    whole = exchanged(sent).reshape(MAIN, -1)
    (input_grad,) = call(
        input_kernel, (out,), [pairs], conv_flops, (flags, source, upstream, grad, g_far, side, w_one_back)
    )
    whole, input_grad = lax.optimization_barrier((whole, input_grad))
    other = lax.ppermute(whole, "core", SWAP)
    owned = jax.ShapeDtypeStruct((channels, 27 * channels // owners), F32)
    first_grad, second_grad = small_call(unpack_kernel, (owned, owned), (flags, whole, other), True)
    return (
        block_output[None],
        input_grad[None],
        first_grad.T,
        second_grad.T,
    )


def solution(mesh):
    shape = mesh.shape
    axes = CLIP_AXES + TIME + ("x_hi",)
    split = Mesh(mesh.devices.reshape(2, shape["dp"] // 2, shape["tm"] // 2, 2, shape["height"]), axes)
    field = P(CLIP_AXES, TIME, "x_hi", None, None)
    return jax.shard_map(
        local,
        mesh=split,
        in_specs=(field, field, P(), P()),
        out_specs=(field, field, P(CLIP_AXES, None), P(CLIP_AXES, None)),
        check_vma=False,
    )
```
